32 devices in a mesh: pipe: 2 (over y), dp: 4 (over z), tensor: 4 (over x, core).
Axes of the slice: x: 2, y: 2, z: 4, core: 2. Of those that a mesh axis runs over, the one named last changes fastest.
Arguments:
- tokens: bfloat16 [3072, 8192], P(('pipe', 'dp'), 'tensor'), parts along dimension 0, may hold values from -6 to 6
- pattern: int32 [128, 6], P('pipe'), parts along dimension 0, may hold values from 0 to 31, as said below
- blocks: bfloat16 [128, 6, 256, 256], P(('pipe', 'tensor'), None, 'dp'), parts along dimension 0, may hold values from -0.15625 to 0.15625
- left_factor: bfloat16 [16384, 512], P(('pipe', 'tensor'), 'dp'), parts along dimension 0, may hold values from -0.0625 to 0.0625
- right_factor: bfloat16 [1024, 16384], P(('pipe', 'dp'), 'tensor'), parts along dimension 0, may hold values from -0.25 to 0.25
- cotangent: bfloat16 [3072, 16384], P(('pipe', 'dp'), 'tensor'), parts along dimension 0, may hold values from -6 to 6
Outputs:
- hidden: bfloat16 [3072, 16384], P(('pipe', 'dp'), 'tensor'), parts along dimension 0
- token_grad: float32 [3072, 8192], P(('pipe', 'dp'), 'tensor'), parts along dimension 0
- block_grad: float32 [128, 6, 256, 256], P(('pipe', 'tensor'), None, 'dp'), parts along dimension 0
- left_grad: float32 [16384, 512], P(('pipe', 'tensor'), 'dp'), parts along dimension 0
- right_grad: float32 [1024, 16384], P(('pipe', 'dp'), 'tensor'), parts along dimension 0
The draws below stay inside these ranges and needn't reach their ends.
There are 2 independent parts, one for each index of `pipe`. The reference program is written for one: setup_inputs(seed, part) draws one part's arguments, and reference() takes and returns one part's arrays. A program takes and returns all parts, laid end to end along the dimension named above; each array names one. Nothing has to cross between parts.
Inputs may be any that keep to these rules, and one draw needn't show every extreme that they name: `pattern`: row j lists the 6 input blocks feeding hidden block j: under a relabeling of the 32 input blocks drawn from the seed, they are the labels of (j mod 32) XOR s for s = 0 and then the powers of two below 32 in rising order; a row's entries are distinct.
All inputs are finite; a program needn't handle non-finite values.
Results may differ from the reference program's by a relative error of at most 0.017.
Values may be sent and summed in bfloat16 or wider, within the bound.
A program may use at most 256 MiB of HBM per device.

```python
import jax
import jax.numpy as jnp
from jax import lax

D = 8192
H = 16384
BS = 256
R = 512
K = 6
TOK_DEV = 384
NBD = 32
NBH = 64
TOKENS = 1536
N_DP = 4
N_TENSOR = 4


def draw_pattern(key, part):
    relabel = jax.random.permutation(key, NBD).astype(jnp.int32)
    column_ids = jnp.arange(NBH, dtype=jnp.int32) % NBD
    slot_ids = jnp.arange(K, dtype=jnp.int32)
    strides = jnp.where(slot_ids == 0, 0, jnp.left_shift(jnp.int32(1), jnp.maximum(slot_ids - 1, 0)))
    return relabel[jnp.bitwise_xor(column_ids[:, None], strides[None, :])]


def block_scale(stream_key, dims, shards, least, top_value):
    level, own = 1.0, jax.random.fold_in(stream_key, 6)
    for dim, shards_of in shards:
        draws = jnp.exp(jax.random.uniform(jax.random.fold_in(own, dim), (shards_of,), jnp.float32, least / len(shards), top_value / len(shards)))
        level = level * jnp.repeat(draws, dims[dim] // shards_of).reshape([-1 if axis == dim else 1 for axis in range(len(dims))])
    return level


def noise(key, extent, spread, limit, split=(), held_as=jnp.bfloat16):
    entries = jax.random.normal(key, extent, jnp.float32) * spread
    if len(split) > 0:
        entries = block_scale(key, extent, split, -0.22, 0.18) * entries
    return jnp.clip(entries, min=-limit, max=limit).astype(held_as)


def setup_inputs(seed: int = 0, part: int = 0) -> dict:
    streams_of = jax.random.split(jax.random.key(seed), 7)
    own_keys = jax.random.split(jax.random.fold_in(streams_of[6], part), 7)
    return {
        "tokens": noise(own_keys[0], (TOKENS, D), 1.0, 6.0, ((0, 4), (1, 4))),
        "pattern": draw_pattern(jax.random.fold_in(jax.random.fold_in(streams_of[6], part), 71), part),
        "blocks": noise(own_keys[2], (NBH, K, BS, BS), (K * BS) ** -0.5, 0.15625, ((0, 4), (2, 4))),
        "left_factor": noise(own_keys[3], (D, R), D ** -0.5, 0.0625, ((0, 4), (1, 4))),
        "right_factor": noise(own_keys[4], (R, H), R ** -0.5, 0.25, ((0, 4), (1, 4))),
        "cotangent": noise(own_keys[5], (TOKENS, H), 1.0, 6.0, ((0, 4), (1, 4))),
    }


SQRT_HALF = 0.7071067811865476
INV_ROOT_TWO_PI = 0.3989422804014327


def gelu_parts(preact):
    normal_cdf = 0.5 * (1.0 + jax.scipy.special.erf(preact * SQRT_HALF))
    return preact * normal_cdf, normal_cdf + preact * jnp.exp(-0.5 * preact * preact) * INV_ROOT_TWO_PI


def rounded_sum(partials):
    rounded = lax.optimization_barrier(partials.astype(jnp.bfloat16))
    return jnp.sum(rounded.astype(jnp.float32), axis=0)


def reference(tokens, pattern, blocks, left_factor, right_factor, cotangent):
    token_count = tokens.shape[0]
    feature_blocks = tokens.reshape(token_count, NBD, BS)
    rank_acts = jnp.dot(tokens, left_factor, preferred_element_type=jnp.float32).astype(jnp.bfloat16)
    columns = jnp.arange(NBH, dtype=jnp.int32)

    def forward_column(column):
        chosen = jnp.take(feature_blocks, pattern[column], axis=1).astype(jnp.float32)
        column_part = jnp.einsum("tkc,kcd->td", chosen, blocks[column].astype(jnp.float32))
        right_cols = lax.dynamic_slice_in_dim(right_factor, column * BS, BS, 1)
        return column_part + jnp.dot(rank_acts, right_cols, preferred_element_type=jnp.float32)

    preact_cols = lax.map(forward_column, columns)
    preact = jnp.transpose(preact_cols, (1, 0, 2)).reshape(token_count, H)
    activated, slope_values = gelu_parts(preact)
    hidden = activated.astype(jnp.bfloat16)
    grad_pre = (cotangent.astype(jnp.float32) * slope_values).astype(jnp.bfloat16)
    rank_grad = jnp.dot(grad_pre, right_factor.T, preferred_element_type=jnp.float32).astype(jnp.bfloat16)

    grouped_rank = rank_acts.reshape(N_DP, TOK_DEV, R).astype(jnp.float32)
    grouped_grad = grad_pre.reshape(N_DP, TOK_DEV, H).astype(jnp.float32)
    right_grad = rounded_sum(jnp.einsum("gtr,gth->grh", grouped_rank, grouped_grad))
    grouped_tokens = tokens.reshape(N_DP, TOK_DEV, D).astype(jnp.float32)
    grouped_rank_grad = rank_grad.reshape(N_DP, TOK_DEV, R).astype(jnp.float32)
    left_grad = rounded_sum(jnp.einsum("gtc,gtr->gcr", grouped_tokens, grouped_rank_grad))

    grad_blocks = grad_pre.reshape(token_count, NBH, BS)

    def block_column(column):
        chosen = jnp.take(feature_blocks, pattern[column], axis=1).reshape(N_DP, TOK_DEV, K, BS).astype(jnp.float32)
        grad_col = grad_blocks[:, column].reshape(N_DP, TOK_DEV, BS).astype(jnp.float32)
        return rounded_sum(jnp.einsum("gtkc,gtd->gkcd", chosen, grad_col))

    block_grad = lax.map(block_column, columns)

    group_cols = NBH // N_TENSOR

    def tensor_group(total, group_index):
        def add_column(running, offset):
            column = group_index * group_cols + offset
            contrib = jnp.einsum("td,kcd->tkc", grad_blocks[:, column].astype(jnp.float32), blocks[column].astype(jnp.float32))
            return running.at[:, pattern[column]].add(contrib), None

        running, _ = lax.scan(add_column, jnp.zeros((token_count, NBD, BS), jnp.float32), jnp.arange(group_cols, dtype=jnp.int32))
        rounded = lax.optimization_barrier(running.astype(jnp.bfloat16))
        return total + rounded.astype(jnp.float32), None

    spread_total, _ = lax.scan(tensor_group, jnp.zeros((token_count, NBD, BS), jnp.float32), jnp.arange(N_TENSOR, dtype=jnp.int32))
    token_grad = spread_total.reshape(token_count, D) + jnp.dot(rank_grad, left_factor.T, preferred_element_type=jnp.float32)
    return hidden, token_grad, block_grad, left_grad, right_grad
```

```python
import functools

import jax
import jax.numpy as jnp
from jax import lax
from jax.experimental import pallas as pl
from jax.experimental.pallas import tpu as pltpu
from jax.sharding import PartitionSpec as P

SQRT_HALF = 0.7071067811865476
INV_ROOT_TWO_PI = 0.3989422804014327
CHUNKS = 4
F32 = jnp.float32
BF16 = jnp.bfloat16


def line_gather(own, n):
    from_left, from_right = {}, {}
    for m in range(1, n):
        right_pairs = [(d, d + 1) for d in range(n - 1) if d - (m - 1) >= 0]
        left_pairs = [(d, d - 1) for d in range(1, n) if d + (m - 1) <= n - 1]
        from_left[m] = lax.ppermute(own if m == 1 else from_left[m - 1], "dp", right_pairs)
        from_right[m] = lax.ppermute(own if m == 1 else from_right[m - 1], "dp", left_pairs)
    return [(from_left[m], from_right[n - m]) for m in range(1, n)]


def line_scatter(terms, n):
    got_left = got_right = None
    for m in range(n - 1, 0, -1):
        right_pairs = [(d, d + 1) for d in range(n - 1) if d + m <= n - 1]
        left_pairs = [(d, d - 1) for d in range(1, n) if d - m >= 0]
        to_right = terms[m] if got_left is None else terms[m] + got_left
        to_left = terms[n - m] if got_right is None else terms[n - m] + got_right
        got_left = lax.ppermute(to_right, "dp", right_pairs)
        got_right = lax.ppermute(to_left, "dp", left_pairs)
    return terms[0].astype(F32) + got_left.astype(F32) + got_right.astype(F32)


def chunk_kernel(n, slots, bs, first, base, where_ref, pattern_ref, x_ref, xt_ref, ra_ref, rat_ref, cot_ref, *rest):
    own_ref = rest[0]
    pairs = [(rest[1 + 2 * i], rest[2 + 2 * i]) for i in range(n - 1)]
    rest = rest[1 + 2 * (n - 1) :]
    if not first:
        acc_in, _ = rest[:2]
        rest = rest[2:]
    hid_ref, acc_ref = rest[:2]
    term_refs = rest[2 : 2 + n]
    w_ref, r_ref, bt_ref = rest[2 + n :]
    step = pl.program_id(0)
    me = where_ref[0]
    cs = bs // n
    rs = ra_ref.shape[1] // n
    width = x_ref.shape[1]

    @pl.when(step == 0)
    def _():
        if first:
            acc_ref[...] = jnp.zeros_like(acc_ref)
        else:
            pltpu.sync_copy(acc_in, acc_ref)

    for m in range(n):
        row = pl.multiple_of(lax.rem(me + n - m, n) * cs, cs)
        for k in range(slots + 1):
            lo, size = k * cs, (cs if k < slots else rs)
            if m == 0:
                piece = own_ref[0, lo : lo + size, :]
            else:
                one, other = pairs[m - 1]
                piece = one[0, lo : lo + size, :] + other[0, lo : lo + size, :]
            if k < slots:
                w_ref[k, pl.ds(row, cs), :] = piece
            else:
                r_ref[m * rs : (m + 1) * rs, :] = piece

    starts = [pl.multiple_of(pattern_ref[base + step, k] * bs, bs) for k in range(slots)]
    preact = jnp.dot(ra_ref[...], r_ref[...], preferred_element_type=F32)
    for k in range(slots):
        preact += jnp.dot(x_ref[:, pl.ds(starts[k], bs)], w_ref[k], preferred_element_type=F32)
    cdf = 0.5 * (1.0 + lax.erf(preact * SQRT_HALF))
    hid_ref[...] = (preact * cdf).astype(BF16)
    slope = cdf + preact * jnp.exp(-0.5 * preact * preact) * INV_ROOT_TWO_PI
    grad = (cot_ref[...].astype(F32) * slope).astype(BF16)

    for k in range(slots):
        bt_ref[k] = jnp.dot(xt_ref[pl.ds(starts[k], bs), :], grad, preferred_element_type=F32).astype(BF16)
    right_term = jnp.dot(rat_ref[...], grad, preferred_element_type=F32).astype(BF16)
    for r in range(n):
        row = pl.multiple_of(lax.rem(me + r, n) * cs, cs)
        m = (n - r) % n
        for k in range(slots):
            term_refs[r][0, k * cs : (k + 1) * cs, :] = bt_ref[k, pl.ds(row, cs), :]
        term_refs[r][0, slots * cs :, :] = right_term[m * rs : (m + 1) * rs, :]
    across = (((1,), (1,)), ((), ()))
    for k in range(slots):
        acc_ref[:, pl.ds(starts[k], bs)] += lax.dot_general(grad, w_ref[k], across, preferred_element_type=F32)
    acc_ref[:, width:] += lax.dot_general(grad, r_ref[...], across, preferred_element_type=F32)


def run_chunk(n, slots, bs, base, cj, where, pattern, x, xt, ra, rat, cot, own, pairs, carried):
    tok = x.shape[0]
    rank = ra.shape[1]
    rows = own.shape[1]
    first = carried is None

    def whole(a):
        return pl.BlockSpec(a.shape, lambda i, *_: (0, 0))

    cols = pl.BlockSpec((tok, bs), lambda i, *_: (0, base + i))
    pack = pl.BlockSpec((1, rows, bs), lambda i, *_: (i, 0, 0))
    pack_own = pl.BlockSpec((1, rows, bs), lambda i, *_: (base + i, 0, 0))
    ins = [x, xt, ra, rat, cot, own] + [a for p in pairs for a in p]
    specs = [whole(x), whole(xt), whole(ra), whole(rat), cols, pack_own] + [pack] * (2 * (n - 1))
    aliases = {}
    if not first:
        aliases = {2 + len(ins): 1, 3 + len(ins): 0}
        ins += list(carried)
        specs += [pl.BlockSpec(memory_space=pl.ANY)] * 2
    acc_shape = (tok, x.shape[1] + rank)
    madds = tok * bs * bs * slots * 3 + tok * rank * bs * 3
    out = pl.pallas_call(
        functools.partial(chunk_kernel, n, slots, bs, first, base),
        grid_spec=pltpu.PrefetchScalarGridSpec(
            num_scalar_prefetch=2,
            grid=(cj,),
            in_specs=specs,
            out_specs=[cols, pl.BlockSpec(acc_shape, lambda i, *_: (0, 0))] + [pack] * n,
            scratch_shapes=[
                pltpu.VMEM((slots, bs, bs), BF16),
                pltpu.VMEM((rank, bs), BF16),
                pltpu.VMEM((slots, bs, bs), BF16),
            ],
        ),
        out_shape=[jax.ShapeDtypeStruct(cot.shape, BF16), jax.ShapeDtypeStruct(acc_shape, F32)]
        + [jax.ShapeDtypeStruct((cj, rows, bs), BF16)] * n,
        input_output_aliases=aliases,
        compiler_params=pltpu.CompilerParams(vmem_limit_bytes=60 * 1024 * 1024),
        cost_estimate=pl.CostEstimate(flops=2 * madds * cj, bytes_accessed=50_000_000, transcendentals=0),
    )(where, pattern, *ins)
    return out[0], out[1], out[2:]


def per_device(tokens, pattern, blocks, left_factor, right_factor, cotangent):
    n = lax.axis_size("dp")
    local_cols, slots, cs, bs = blocks.shape
    rs = right_factor.shape[0]
    rw = left_factor.shape[1]
    cj = local_cols // CHUNKS
    me = lax.axis_index("dp").astype(jnp.int32).reshape(1)
    local_pattern = lax.dynamic_slice_in_dim(pattern, lax.axis_index("tensor") * local_cols, local_cols, 0)

    left_pairs = line_gather(left_factor, n)
    packed = jnp.concatenate(
        [blocks.reshape(local_cols, slots * cs, bs), right_factor.reshape(rs, local_cols, bs).transpose(1, 0, 2)], axis=1
    )
    gathered = [line_gather(packed[c * cj : (c + 1) * cj], n) for c in range(CHUNKS)]

    x = lax.all_gather(tokens, "tensor", axis=1, tiled=True)
    xt = x.T
    left_rot = jnp.concatenate([left_factor] + [a + b for a, b in left_pairs], axis=1)
    rank_acts = lax.psum(jnp.dot(tokens, left_rot, preferred_element_type=F32), "tensor").astype(BF16)
    rank_acts_t = rank_acts.T

    carried = None
    sums = []
    for c in range(CHUNKS):
        hidden, acc, terms = run_chunk(
            n, slots, bs, c * cj, cj, me, local_pattern, x, xt, rank_acts, rank_acts_t, cotangent, packed, gathered[c], carried
        )
        carried = (acc, hidden)
        sums.append(line_scatter(list(terms), n))

    width = x.shape[1]
    rank_grad = lax.psum(acc[:, width:].astype(BF16), "tensor")
    token_part = lax.psum_scatter(acc[:, :width].astype(BF16), "tensor", scatter_dimension=1, tiled=True).astype(F32)
    left_term = lax.dot_general(tokens, rank_grad, (((0,), (0,)), ((), ())), preferred_element_type=F32).astype(BF16)
    left_terms = [left_term[:, ((n - r) % n) * rw : ((n - r) % n + 1) * rw] for r in range(n)]
    left_grad = line_scatter(left_terms, n)
    token_grad = token_part + lax.dot_general(
        rank_grad, left_rot, (((1,), (1,)), ((), ())), preferred_element_type=F32
    )
    block_grad = jnp.concatenate([s[:, : slots * cs].reshape(cj, slots, cs, bs) for s in sums], axis=0)
    right_grad = jnp.concatenate([s[:, slots * cs :].transpose(1, 0, 2).reshape(rs, cj * bs) for s in sums], axis=1)
    return (hidden, token_grad, block_grad, left_grad, right_grad)


def solution(mesh):
    placed = (
        P(("pipe", "dp"), "tensor"),
        P("pipe", None),
        P(("pipe", "tensor"), None, "dp", None),
        P(("pipe", "tensor"), "dp"),
        P(("pipe", "dp"), "tensor"),
        P(("pipe", "dp"), "tensor"),
    )
    return jax.shard_map(
        per_device,
        mesh=mesh,
        in_specs=placed,
        out_specs=(
            P(("pipe", "dp"), "tensor"),
            P(("pipe", "dp"), "tensor"),
            P(("pipe", "tensor"), None, "dp", None),
            P(("pipe", "tensor"), "dp"),
            P(("pipe", "dp"), "tensor"),
        ),
        check_vma=False,
    )
```

```python
import functools

import jax
import jax.numpy as jnp
from jax import lax
from jax.experimental import pallas as pl
from jax.experimental.pallas import tpu as pltpu
from jax.sharding import PartitionSpec as P

SQRT_HALF = 0.7071067811865476
INV_ROOT_TWO_PI = 0.3989422804014327
CHUNKS = 4
F32 = jnp.float32
BF16 = jnp.bfloat16


def after(index, *arrays):
    for a in arrays:
        corner = a[(0,) * a.ndim]
        index = index + (corner != corner).astype(jnp.int32)
    return index


def line_gather(own, n):
    from_left, from_right = {}, {}
    for m in range(1, n):
        right_pairs = [(d, d + 1) for d in range(n - 1) if d - (m - 1) >= 0]
        left_pairs = [(d, d - 1) for d in range(1, n) if d + (m - 1) <= n - 1]
        from_left[m] = lax.ppermute(own if m == 1 else from_left[m - 1], "dp", right_pairs)
        from_right[m] = lax.ppermute(own if m == 1 else from_right[m - 1], "dp", left_pairs)
    late = max(1, n - 2)
    return [(from_left[m], from_right[n - m]) for m in range(1, n)], (from_left[late], from_right[late])


def line_scatter(terms, n):
    got_left = got_right = None
    steps = []
    for m in range(n - 1, 0, -1):
        right_pairs = [(d, d + 1) for d in range(n - 1) if d + m <= n - 1]
        left_pairs = [(d, d - 1) for d in range(1, n) if d - m >= 0]
        to_right = terms[m] if got_left is None else terms[m] + got_left
        to_left = terms[n - m] if got_right is None else terms[n - m] + got_right
        got_left = lax.ppermute(to_right, "dp", right_pairs)
        got_right = lax.ppermute(to_left, "dp", left_pairs)
        steps.append((got_left, got_right))
    return terms[0].astype(F32) + got_left.astype(F32) + got_right.astype(F32), steps


def chunk_kernel(n, slots, bs, first, base, where_ref, pattern_ref, x_ref, xt_ref, ra_ref, rat_ref, cot_ref, *rest):
    own_ref = rest[0]
    pairs = [(rest[1 + 2 * i], rest[2 + 2 * i]) for i in range(n - 1)]
    rest = rest[1 + 2 * (n - 1) :]
    if not first:
        acc_in, _ = rest[:2]
        rest = rest[2:]
    hid_ref, acc_ref = rest[:2]
    term_refs = rest[2 : 2 + n]
    w_ref, r_ref, bt_ref = rest[2 + n :]
    step = pl.program_id(0)
    me = where_ref[0]
    cs = bs // n
    rs = ra_ref.shape[1] // n
    width = x_ref.shape[1]

    @pl.when(step == 0)
    def _():
        if first:
            acc_ref[...] = jnp.zeros_like(acc_ref)
        else:
            pltpu.sync_copy(acc_in, acc_ref)

    for m in range(n):
        row = pl.multiple_of(lax.rem(me + n - m, n) * cs, cs)
        for k in range(slots + 1):
            lo, size = k * cs, (cs if k < slots else rs)
            if m == 0:
                piece = own_ref[0, lo : lo + size, :]
            else:
                one, other = pairs[m - 1]
                piece = one[0, lo : lo + size, :] + other[0, lo : lo + size, :]
            if k < slots:
                w_ref[k, pl.ds(row, cs), :] = piece
            else:
                r_ref[m * rs : (m + 1) * rs, :] = piece

    starts = [pl.multiple_of(pattern_ref[base + step, k] * bs, bs) for k in range(slots)]
    preact = jnp.dot(ra_ref[...], r_ref[...], preferred_element_type=F32)
    for k in range(slots):
        preact += jnp.dot(x_ref[:, pl.ds(starts[k], bs)], w_ref[k], preferred_element_type=F32)
    cdf = 0.5 * (1.0 + lax.erf(preact * SQRT_HALF))
    hid_ref[...] = (preact * cdf).astype(BF16)
    slope = cdf + preact * jnp.exp(-0.5 * preact * preact) * INV_ROOT_TWO_PI
    grad = (cot_ref[...].astype(F32) * slope).astype(BF16)

    for k in range(slots):
        bt_ref[k] = jnp.dot(xt_ref[pl.ds(starts[k], bs), :], grad, preferred_element_type=F32).astype(BF16)
    right_term = jnp.dot(rat_ref[...], grad, preferred_element_type=F32).astype(BF16)
    for r in range(n):
        row = pl.multiple_of(lax.rem(me + r, n) * cs, cs)
        m = (n - r) % n
        for k in range(slots):
            term_refs[r][0, k * cs : (k + 1) * cs, :] = bt_ref[k, pl.ds(row, cs), :]
        term_refs[r][0, slots * cs :, :] = right_term[m * rs : (m + 1) * rs, :]
    across = (((1,), (1,)), ((), ()))
    for k in range(slots):
        acc_ref[:, pl.ds(starts[k], bs)] += lax.dot_general(grad, w_ref[k], across, preferred_element_type=F32)
    acc_ref[:, width:] += lax.dot_general(grad, r_ref[...], across, preferred_element_type=F32)


def run_chunk(n, slots, bs, base, cj, where, pattern, x, xt, ra, rat, cot, own, pairs, carried):
    tok = x.shape[0]
    rank = ra.shape[1]
    rows = own.shape[1]
    first = carried is None

    def whole(a):
        return pl.BlockSpec(a.shape, lambda i, *_: (0, 0))

    cols = pl.BlockSpec((tok, bs), lambda i, *_: (0, base + i))
    pack = pl.BlockSpec((1, rows, bs), lambda i, *_: (i, 0, 0))
    pack_own = pl.BlockSpec((1, rows, bs), lambda i, *_: (base + i, 0, 0))
    ins = [x, xt, ra, rat, cot, own] + [a for p in pairs for a in p]
    specs = [whole(x), whole(xt), whole(ra), whole(rat), cols, pack_own] + [pack] * (2 * (n - 1))
    aliases = {}
    if not first:
        aliases = {2 + len(ins): 1, 3 + len(ins): 0}
        ins += list(carried)
        specs += [pl.BlockSpec(memory_space=pl.ANY)] * 2
    acc_shape = (tok, x.shape[1] + rank)
    madds = tok * bs * bs * slots * 3 + tok * rank * bs * 3
    out = pl.pallas_call(
        functools.partial(chunk_kernel, n, slots, bs, first, base),
        grid_spec=pltpu.PrefetchScalarGridSpec(
            num_scalar_prefetch=2,
            grid=(cj,),
            in_specs=specs,
            out_specs=[cols, pl.BlockSpec(acc_shape, lambda i, *_: (0, 0))] + [pack] * n,
            scratch_shapes=[
                pltpu.VMEM((slots, bs, bs), BF16),
                pltpu.VMEM((rank, bs), BF16),
                pltpu.VMEM((slots, bs, bs), BF16),
            ],
        ),
        out_shape=[jax.ShapeDtypeStruct(cot.shape, BF16), jax.ShapeDtypeStruct(acc_shape, F32)]
        + [jax.ShapeDtypeStruct((cj, rows, bs), BF16)] * n,
        input_output_aliases=aliases,
        compiler_params=pltpu.CompilerParams(vmem_limit_bytes=60 * 1024 * 1024),
        cost_estimate=pl.CostEstimate(flops=2 * madds * cj, bytes_accessed=50_000_000, transcendentals=0),
    )(where, pattern, *ins)
    return out[0], out[1], out[2:]


def per_device(tokens, pattern, blocks, left_factor, right_factor, cotangent):
    n = lax.axis_size("dp")
    local_cols, slots, cs, bs = blocks.shape
    rs = right_factor.shape[0]
    rw = left_factor.shape[1]
    cj = local_cols // CHUNKS
    me = lax.axis_index("dp").astype(jnp.int32).reshape(1)
    local_pattern = lax.dynamic_slice_in_dim(pattern, lax.axis_index("tensor") * local_cols, local_cols, 0)

    left_pairs, _ = line_gather(left_factor, n)
    packed = jnp.concatenate(
        [blocks.reshape(local_cols, slots * cs, bs), right_factor.reshape(rs, local_cols, bs).transpose(1, 0, 2)], axis=1
    )
    gathered = []
    waits = ()
    for c in range(CHUNKS):
        part = lax.dynamic_slice_in_dim(packed, after(jnp.int32(c * cj), *waits), cj, 0)
        pairs, waits = line_gather(part, n)
        gathered.append(pairs)

    x = lax.all_gather(tokens, "tensor", axis=1, tiled=True)
    xt = x.T
    left_rot = jnp.concatenate([left_factor] + [a + b for a, b in left_pairs], axis=1)
    rank_acts = lax.psum(jnp.dot(tokens, left_rot, preferred_element_type=F32), "tensor").astype(BF16)
    rank_acts_t = rank_acts.T

    carried = None
    sums = []
    steps = []
    for c in range(CHUNKS):
        where = me
        if c >= 1:
            where = after(where, *steps[c - 1][0])
        if c >= 2:
            where = after(where, *steps[c - 2][-1])
        hidden, acc, terms = run_chunk(
            n, slots, bs, c * cj, cj, where, local_pattern, x, xt, rank_acts, rank_acts_t, cotangent, packed, gathered[c], carried
        )
        carried = (acc, hidden)
        total, got = line_scatter(list(terms), n)
        sums.append(total)
        steps.append(got)

    width = x.shape[1]
    rank_grad = lax.psum(acc[:, width:].astype(BF16), "tensor")
    token_part = lax.psum_scatter(acc[:, :width].astype(BF16), "tensor", scatter_dimension=1, tiled=True).astype(F32)
    left_term = lax.dot_general(tokens, rank_grad, (((0,), (0,)), ((), ())), preferred_element_type=F32).astype(BF16)
    left_terms = [left_term[:, ((n - r) % n) * rw : ((n - r) % n + 1) * rw] for r in range(n)]
    left_grad, _ = line_scatter(left_terms, n)
    token_grad = token_part + lax.dot_general(
        rank_grad, left_rot, (((1,), (1,)), ((), ())), preferred_element_type=F32
    )
    block_grad = jnp.concatenate([s[:, : slots * cs].reshape(cj, slots, cs, bs) for s in sums], axis=0)
    right_grad = jnp.concatenate([s[:, slots * cs :].transpose(1, 0, 2).reshape(rs, cj * bs) for s in sums], axis=1)
    return (hidden, token_grad, block_grad, left_grad, right_grad)


def solution(mesh):
    placed = (
        P(("pipe", "dp"), "tensor"),
        P("pipe", None),
        P(("pipe", "tensor"), None, "dp", None),
        P(("pipe", "tensor"), "dp"),
        P(("pipe", "dp"), "tensor"),
        P(("pipe", "dp"), "tensor"),
    )
    return jax.shard_map(
        per_device,
        mesh=mesh,
        in_specs=placed,
        out_specs=(
            P(("pipe", "dp"), "tensor"),
            P(("pipe", "dp"), "tensor"),
            P(("pipe", "tensor"), None, "dp", None),
            P(("pipe", "tensor"), "dp"),
            P(("pipe", "dp"), "tensor"),
        ),
        check_vma=False,
    )
```

```python
import functools

import jax
import jax.numpy as jnp
from jax import lax
from jax.experimental import pallas as pl
from jax.experimental.pallas import tpu as pltpu
from jax.sharding import PartitionSpec as P

SQRT_HALF = 0.7071067811865476
INV_ROOT_TWO_PI = 0.3989422804014327
CHUNKS = 3
F32 = jnp.float32
BF16 = jnp.bfloat16


def after(index, *arrays):
    for a in arrays:
        corner = a[(0,) * a.ndim]
        index = index + (corner != corner).astype(jnp.int32)
    return index


def line_gather(own, n):
    from_left, from_right = {}, {}
    for m in range(1, n):
        right_pairs = [(d, d + 1) for d in range(n - 1) if d - (m - 1) >= 0]
        left_pairs = [(d, d - 1) for d in range(1, n) if d + (m - 1) <= n - 1]
        from_left[m] = lax.ppermute(own if m == 1 else from_left[m - 1], "dp", right_pairs)
        from_right[m] = lax.ppermute(own if m == 1 else from_right[m - 1], "dp", left_pairs)
    late = max(1, n - 2)
    return [(from_left[m], from_right[n - m]) for m in range(1, n)], (from_left[late], from_right[late])


def line_scatter(terms, n):
    got_left = got_right = None
    steps = []
    for m in range(n - 1, 0, -1):
        right_pairs = [(d, d + 1) for d in range(n - 1) if d + m <= n - 1]
        left_pairs = [(d, d - 1) for d in range(1, n) if d - m >= 0]
        to_right = terms[m] if got_left is None else terms[m] + got_left
        to_left = terms[n - m] if got_right is None else terms[n - m] + got_right
        got_left = lax.ppermute(to_right, "dp", right_pairs)
        got_right = lax.ppermute(to_left, "dp", left_pairs)
        steps.append((got_left, got_right))
    return terms[0].astype(F32) + got_left.astype(F32) + got_right.astype(F32), steps


def chunk_kernel(n, slots, bs, first, last, base, where_ref, pattern_ref, x_ref, xt_ref, ra_ref, rat_ref, cot_ref, *rest):
    own_ref = rest[0]
    pairs = [(rest[1 + 2 * i], rest[2 + 2 * i]) for i in range(n - 1)]
    rest = rest[1 + 2 * (n - 1) :]
    if not first:
        acc_in, _ = rest[:2]
        rest = rest[2:]
    if last:
        hid_ref, spread_ref, rank_ref = rest[:3]
        term_refs = rest[3 : 3 + n]
        w_ref, r_ref, bt_ref, acc_ref = rest[3 + n :]
    else:
        hid_ref, acc_ref = rest[:2]
        term_refs = rest[2 : 2 + n]
        w_ref, r_ref, bt_ref = rest[2 + n :]
    step = pl.program_id(0)
    me = where_ref[0]
    cs = bs // n
    rs = ra_ref.shape[1] // n
    width = x_ref.shape[1]

    @pl.when(step == 0)
    def _():
        if first:
            acc_ref[...] = jnp.zeros_like(acc_ref)
        else:
            pltpu.sync_copy(acc_in, acc_ref)

    for m in range(n):
        row = pl.multiple_of(lax.rem(me + n - m, n) * cs, cs)
        for k in range(slots + 1):
            lo, size = k * cs, (cs if k < slots else rs)
            if m == 0:
                piece = own_ref[0, lo : lo + size, :]
            else:
                one, other = pairs[m - 1]
                piece = one[0, lo : lo + size, :] + other[0, lo : lo + size, :]
            if k < slots:
                w_ref[k, pl.ds(row, cs), :] = piece
            else:
                r_ref[m * rs : (m + 1) * rs, :] = piece

    starts = [pl.multiple_of(pattern_ref[base + step, k] * bs, bs) for k in range(slots)]
    preact = jnp.dot(ra_ref[...], r_ref[...], preferred_element_type=F32)
    for k in range(slots):
        preact += jnp.dot(x_ref[:, pl.ds(starts[k], bs)], w_ref[k], preferred_element_type=F32)
    cdf = 0.5 * (1.0 + lax.erf(preact * SQRT_HALF))
    hid_ref[...] = (preact * cdf).astype(BF16)
    slope = cdf + preact * jnp.exp(-0.5 * preact * preact) * INV_ROOT_TWO_PI
    grad = (cot_ref[...].astype(F32) * slope).astype(BF16)

    for k in range(slots):
        bt_ref[k] = jnp.dot(xt_ref[pl.ds(starts[k], bs), :], grad, preferred_element_type=F32).astype(BF16)
    right_term = jnp.dot(rat_ref[...], grad, preferred_element_type=F32).astype(BF16)
    for r in range(n):
        row = pl.multiple_of(lax.rem(me + r, n) * cs, cs)
        m = (n - r) % n
        for k in range(slots):
            term_refs[r][0, k * cs : (k + 1) * cs, :] = bt_ref[k, pl.ds(row, cs), :]
        term_refs[r][0, slots * cs :, :] = right_term[m * rs : (m + 1) * rs, :]
    across = (((1,), (1,)), ((), ()))
    for k in range(slots):
        acc_ref[:, pl.ds(starts[k], bs)] += lax.dot_general(grad, w_ref[k], across, preferred_element_type=F32)
    acc_ref[:, width:] += lax.dot_general(grad, r_ref[...], across, preferred_element_type=F32)
    if last:

        @pl.when(step == pl.num_programs(0) - 1)
        def _():
            spread_ref[...] = acc_ref[:, :width].astype(BF16)
            rank_ref[...] = acc_ref[:, width:].astype(BF16)


def run_chunk(n, slots, bs, base, cj, last, where, pattern, x, xt, ra, rat, cot, own, pairs, carried):
    tok = x.shape[0]
    rank = ra.shape[1]
    rows = own.shape[1]
    first = carried is None

    def whole(a):
        return pl.BlockSpec(a.shape, lambda i, *_: (0, 0), pipeline_mode=pl.Buffered(1))

    cols = pl.BlockSpec((tok, bs), lambda i, *_: (0, base + i))
    pack = pl.BlockSpec((1, rows, bs), lambda i, *_: (i, 0, 0))
    pack_own = pl.BlockSpec((1, rows, bs), lambda i, *_: (base + i, 0, 0))
    ins = [x, xt, ra, rat, cot, own] + [a for p in pairs for a in p]
    specs = [whole(x), whole(xt), whole(ra), whole(rat), cols, pack_own] + [pack] * (2 * (n - 1))
    aliases = {}
    if not first:
        aliases = {3 + len(ins): 0} if last else {2 + len(ins): 1, 3 + len(ins): 0}
        ins += list(carried)
        specs += [pl.BlockSpec(memory_space=pl.ANY)] * 2
    acc_shape = (tok, x.shape[1] + rank)
    if last:
        sums = [(tok, x.shape[1]), (tok, rank)]
        sum_type = BF16
    else:
        sums = [acc_shape]
        sum_type = F32
    madds = tok * bs * bs * slots * 3 + tok * rank * bs * 3
    out = pl.pallas_call(
        functools.partial(chunk_kernel, n, slots, bs, first, last, base),
        grid_spec=pltpu.PrefetchScalarGridSpec(
            num_scalar_prefetch=2,
            grid=(cj,),
            in_specs=specs,
            out_specs=[cols] + [pl.BlockSpec(shape, lambda i, *_: (0, 0)) for shape in sums] + [pack] * n,
            scratch_shapes=[
                pltpu.VMEM((slots, bs, bs), BF16),
                pltpu.VMEM((rank, bs), BF16),
                pltpu.VMEM((slots, bs, bs), BF16),
            ]
            + ([pltpu.VMEM(acc_shape, F32)] if last else []),
        ),
        out_shape=[jax.ShapeDtypeStruct(cot.shape, BF16)]
        + [jax.ShapeDtypeStruct(shape, sum_type) for shape in sums]
        + [jax.ShapeDtypeStruct((cj, rows, bs), BF16)] * n,
        input_output_aliases=aliases,
        compiler_params=pltpu.CompilerParams(vmem_limit_bytes=60 * 1024 * 1024),
        cost_estimate=pl.CostEstimate(flops=2 * madds * cj, bytes_accessed=50_000_000, transcendentals=0),
    )(where, pattern, *ins)
    return out[0], out[1 : 1 + len(sums)], out[1 + len(sums) :]


def per_device(tokens, pattern, blocks, left_factor, right_factor, cotangent):
    n = lax.axis_size("dp")
    local_cols, slots, cs, bs = blocks.shape
    rs = right_factor.shape[0]
    rw = left_factor.shape[1]
    bounds = [-(-local_cols * c // CHUNKS) for c in range(CHUNKS + 1)]
    me = lax.axis_index("dp").astype(jnp.int32).reshape(1)
    local_pattern = lax.dynamic_slice_in_dim(pattern, lax.axis_index("tensor") * local_cols, local_cols, 0)

    left_pairs, waits = line_gather(left_factor, n)
    packed = jnp.concatenate(
        [blocks.reshape(local_cols, slots * cs, bs), right_factor.reshape(rs, local_cols, bs).transpose(1, 0, 2)], axis=1
    )
    gathered = []
    for c in range(CHUNKS):
        lo, hi = bounds[c : c + 2]
        part = lax.dynamic_slice_in_dim(packed, after(jnp.int32(lo), *waits), hi - lo, 0)
        pairs, waits = line_gather(part, n)
        gathered.append(pairs)

    x = lax.all_gather(tokens, "tensor", axis=1, tiled=True)
    xt = x.T
    left_rot = jnp.concatenate([left_factor] + [a + b for a, b in left_pairs], axis=1)
    rank_acts = lax.psum(jnp.dot(tokens, left_rot, preferred_element_type=F32), "tensor").astype(BF16)
    rank_acts_t = rank_acts.T

    carried = None
    sums = []
    steps = []
    for c in range(CHUNKS):
        where = me
        if c >= 1:
            where = after(where, *steps[c - 1][0])
        if c >= 2:
            where = after(where, *steps[c - 2][-1])
        lo, hi = bounds[c : c + 2]
        hidden, acc, terms = run_chunk(
            n, slots, bs, lo, hi - lo, c == CHUNKS - 1, where, local_pattern, x, xt, rank_acts, rank_acts_t, cotangent, packed, gathered[c], carried
        )
        carried = (acc[0], hidden)
        total, got = line_scatter(list(terms), n)
        sums.append(total)
        steps.append(got)

    rank_grad = lax.psum(acc[1], "tensor")
    token_part = lax.psum_scatter(acc[0], "tensor", scatter_dimension=1, tiled=True).astype(F32)
    left_term = lax.dot_general(tokens, rank_grad, (((0,), (0,)), ((), ())), preferred_element_type=F32).astype(BF16)
    left_terms = [left_term[:, ((n - r) % n) * rw : ((n - r) % n + 1) * rw] for r in range(n)]
    left_grad, _ = line_scatter(left_terms, n)
    token_grad = token_part + lax.dot_general(
        rank_grad, left_rot, (((1,), (1,)), ((), ())), preferred_element_type=F32
    )
    block_grad = jnp.concatenate([s[:, : slots * cs].reshape(-1, slots, cs, bs) for s in sums], axis=0)
    right_grad = jnp.concatenate([s[:, slots * cs :].transpose(1, 0, 2).reshape(rs, -1) for s in sums], axis=1)
    return (hidden, token_grad, block_grad, left_grad, right_grad)


def solution(mesh):
    placed = (
        P(("pipe", "dp"), "tensor"),
        P("pipe", None),
        P(("pipe", "tensor"), None, "dp", None),
        P(("pipe", "tensor"), "dp"),
        P(("pipe", "dp"), "tensor"),
        P(("pipe", "dp"), "tensor"),
    )
    return jax.shard_map(
        per_device,
        mesh=mesh,
        in_specs=placed,
        out_specs=(
            P(("pipe", "dp"), "tensor"),
            P(("pipe", "dp"), "tensor"),
            P(("pipe", "tensor"), None, "dp", None),
            P(("pipe", "tensor"), "dp"),
            P(("pipe", "dp"), "tensor"),
        ),
        check_vma=False,
    )
```
